32 devices in a mesh: rows: 16 (over z, x, core), rhs: 2 (over y).
Axes of the slice: x: 2, y: 2, z: 4, core: 2. Of those that a mesh axis runs over, the one named last changes fastest.
Arguments:
- obs_points: int32 [2, 1, 8192], P(None, None, 'rows'), may hold values from 0 to 255
- pred_points: int32 [2, 2048], P(None, 'rhs'), may hold values from 0 to 255
- factor_panels: bfloat16 [1, 8192, 2, 512], P(None, ('rows', 'rhs')), may hold values from -0.25 to 0.25
- diag_inverse: bfloat16 [2, 512, 512], P(None, 'rhs'), as said below
Outputs:
- updated: bfloat16 [1, 8192, 2048], P(None, 'rows', 'rhs')
The draws below stay inside these ranges and needn't reach their ends.
Inputs may be any that keep to these rules, and one draw needn't show every extreme that they name: `diag_inverse`: lower triangular.
All inputs are finite; a program needn't handle non-finite values.
Results may differ from the reference program's by a relative error of at most 0.006.
Values may be sent and summed in bfloat16 or wider, within the bound.
A program may use at most 64 MiB of HBM per device.

```python
import math
import jax
import jax.numpy as jnp
from jax import lax

BS = 512
ROWS_DEV = 1
GRID = 256
SCALE = 16
NBLK = 16
PRED = 2048
N_ROWS = 16


def draw_diag_inverse(key, part):
    key = jax.random.fold_in(key, 5)
    key_lower, key_diag = jax.random.split(key, 2)
    row_index = jnp.arange(BS)[:, None]
    col_index = jnp.arange(BS)[None, :]
    lower = 0.5 * jax.random.normal(key_lower, (2, BS, BS), jnp.float32) / math.sqrt(BS)
    diagonal = jnp.exp(jax.random.uniform(key_diag, (2, BS), jnp.float32, math.log(0.7), math.log(1.4)))
    lower_part = jnp.where(row_index > col_index, lower, 0.0)
    diag_part = jnp.where(row_index == col_index, diagonal[:, :, None], 0.0)
    return (lower_part + diag_part).astype(jnp.bfloat16)


def with_ends(array, rng, smallest, largest):
    shape = array.shape
    place = [jax.random.randint(jax.random.fold_in(rng, axis), (), 0, shape[axis]) for axis in range(len(shape))]
    array = array.at[tuple(place)].set(smallest)
    longest = shape.index(max(shape))
    place[longest] = (place[longest] + 1) % shape[longest]
    return array.at[tuple(place)].set(largest)


def block_levels(stream_key, extent, shards, low, top_value):
    def one(position, shards_of):
        steps = jax.random.uniform(jax.random.fold_in(jax.random.fold_in(stream_key, 6), position), (shards_of,), jnp.float32, low / len(shards), top_value / len(shards))
        return jnp.repeat(jnp.exp(steps), extent[position] // shards_of).reshape((-1,) + (1,) * (len(extent) - position - 1))

    gain = one(*shards[0])
    for cut in shards[1:]:
        gain = gain * one(*cut)
    return gain


def centred(key, shape, width, reach, cuts=(), dtype=jnp.bfloat16):
    array = jax.random.normal(key, shape, jnp.float32) * width
    if len(cuts) > 0:
        array = block_levels(key, shape, cuts, -0.22, 0.18) * array
    return jnp.clip(array, min=-reach, max=reach).astype(dtype)


def setup_inputs(seed: int = 0) -> dict:
    streams_of = jax.random.split(jax.random.key(seed), 5)
    obs_points = with_ends(jax.random.randint(streams_of[0], (2, ROWS_DEV, N_ROWS * BS), 0, GRID), jax.random.fold_in(streams_of[0], 1), 0, GRID - 1).astype(jnp.int32)
    pred_points = with_ends(jax.random.randint(streams_of[1], (2, PRED), 0, GRID), jax.random.fold_in(streams_of[1], 1), 0, GRID - 1).astype(jnp.int32)
    factor_panels = centred(streams_of[2], (ROWS_DEV, N_ROWS * BS, 2, BS), BS ** -0.5, 0.25, ((1, 32),))
    diag_inverse = draw_diag_inverse(jax.random.fold_in(streams_of[4], 71), 0)
    return dict(obs_points=obs_points, pred_points=pred_points, factor_panels=factor_panels, diag_inverse=diag_inverse)


sill_level = 8.0

def covariance(points, targets):
    delta_x = points[0][..., None] - targets[0]
    delta_y = points[1][..., None] - targets[1]
    distance = jnp.sqrt(delta_x * delta_x + delta_y * delta_y)
    scaled = math.sqrt(3.0) / SCALE * distance
    return sill_level * (1.0 + scaled) * jnp.exp(-scaled)

def reference(obs_points, pred_points, factor_panels, diag_inverse):
    targets = pred_points.astype(jnp.float32)
    points = obs_points.astype(jnp.float32).reshape(2, ROWS_DEV, N_ROWS, BS)
    panels = factor_panels.reshape(ROWS_DEV, N_ROWS, BS, 2, BS)
    first_rhs = covariance(points[:, 0, 0], targets).astype(jnp.bfloat16)
    first_solved = jnp.dot(diag_inverse[0], first_rhs, preferred_element_type=jnp.float32).astype(jnp.bfloat16)
    second_total = covariance(points[:, 0, 1], targets) - jnp.dot(panels[0, 1, :, 0, :], first_solved, preferred_element_type=jnp.float32)
    second_rhs = second_total.astype(jnp.bfloat16)
    second_solved = jnp.dot(diag_inverse[1], second_rhs, preferred_element_type=jnp.float32).astype(jnp.bfloat16)

    def update_block(inputs_pair):
        block_points, tile_pair = inputs_pair
        total = covariance(block_points, targets)
        total = total - jnp.dot(tile_pair[:, 0, :], first_solved, preferred_element_type=jnp.float32)
        total = total - jnp.dot(tile_pair[:, 1, :], second_solved, preferred_element_type=jnp.float32)
        return total.astype(jnp.bfloat16)
    flat_points = points.transpose(1, 2, 0, 3).reshape(NBLK, 2, BS)
    flat_panels = panels.reshape(NBLK, BS, 2, BS)
    blocks = lax.map(update_block, (flat_points, flat_panels))
    blocks = blocks.at[0].set(first_solved).at[1].set(second_solved)
    return blocks.reshape(ROWS_DEV, N_ROWS * BS, PRED)
```

```python
import functools
import math

import jax
import jax.numpy as jnp
from jax import lax
from jax.experimental import pallas as pl
from jax.experimental.pallas import tpu as pltpu
from jax.sharding import PartitionSpec as P

SCALE = 16
SILL = 8.0
LANES = 4
PIECES = 2
RATE = math.sqrt(3.0) / SCALE * math.log2(math.e)
SLOPE = SILL * math.log(2.0)
MESH = pl.DeviceIdType.MESH


def covariance(px, py, ox, oy):
    dx = ox - px
    dy = oy - py
    square = dx * dx + dy * dy
    scaled = (square * RATE) * lax.rsqrt(jnp.maximum(square, 1e-6))
    return (SILL + SLOPE * scaled) * jnp.exp2(-scaled)


def kernel(
    n_rows, n_rhs, obs_ref, pred_ref, panel_ref, inv_ref, out_ref,
    head, tiles, solved, base, first_rhs, second_base, lead_pts, columns, result,
    local_sem, send_sem, recv_sem,
):
    r = lax.axis_index("rows")
    c = lax.axis_index("rhs")
    bs = head.shape[1]
    q = bs // n_rhs
    w = q // LANES
    lane = lax.rem(r, LANES)
    hop = r // LANES
    hops = n_rows // LANES
    x_side = r + 2 - 4 * (lane // 2)
    c_side = r + 1 - 2 * lax.rem(lane, 2)
    x_lane = lax.rem(x_side, LANES)
    c_lane = lax.rem(c_side, LANES)
    d_lane = lax.rem(c_lane + 2, LANES)
    is_first = r == 0
    is_second = r == 1
    updates = r >= 2

    send_count = [0]
    recv_count = [0]

    def slot(count):
        count[0] += 1
        return count[0] - 1

    def link(src, dst, row, side, send=None, recv=None):
        return pltpu.make_async_remote_copy(
            src_ref=src, dst_ref=dst,
            send_sem=send_sem.at[slot(send_count) if send is None else send],
            recv_sem=recv_sem.at[slot(recv_count) if recv is None else recv],
            device_id=(row, side), device_id_type=MESH,
        )

    def rows_of(side, which):
        return pl.ds(pl.multiple_of(side * q + which * w, w), w)

    def chunk(side):
        return pl.ds(pl.multiple_of(side * q, q), q)

    own = chunk(c)
    copy_inv = pltpu.make_async_copy(inv_ref, head.at[0:2, own], local_sem.at[0])
    copy_tiles = pltpu.make_async_copy(panel_ref, tiles.at[:, own], local_sem.at[1])
    copy_lower = pltpu.make_async_copy(
        panel_ref.at[0, pl.ds(w, w)], head.at[2, rows_of(c, 1)], local_sem.at[2]
    )
    copy_inv.start()
    copy_tiles.start()

    @pl.when(is_second)
    def _():
        copy_lower.start()

    barrier = pltpu.get_barrier_semaphore()
    first_of_hop = hop * LANES
    for dl in range(LANES):
        for dc in range(n_rhs):
            if dl == 0 and dc == 0:
                continue
            pl.semaphore_signal(
                barrier, inc=1, device_id_type=MESH,
                device_id=(first_of_hop + lax.rem(lane + dl, LANES), lax.rem(c + dc, n_rhs)),
            )
    has_next = hop < hops - 1
    has_prev = hop > 0

    @pl.when(has_next)
    def _():
        pl.semaphore_signal(barrier, inc=1, device_id=(r + LANES, c), device_id_type=MESH)

    @pl.when(has_prev)
    def _():
        pl.semaphore_signal(barrier, inc=1, device_id=(r - LANES, c), device_id_type=MESH)

    neighbours = has_next.astype(jnp.int32) + has_prev.astype(jnp.int32)
    pl.semaphore_wait(barrier, LANES * n_rhs - 1 + neighbours)

    point_recv = [slot(recv_count) for _ in range(2)]
    point_copies = []
    for block in range(2):
        sends = []
        for other in range(LANES):
            if other != block:
                sends.append(link(obs_ref, lead_pts.at[block], other, c, recv=point_recv[block]))
        point_copies.append(sends)

        @pl.when(r == block)
        def _():
            for copy in sends:
                copy.start()

    inv_copies = []
    inv_recv = []
    for d in range(1, n_rhs):
        inv_recv.append(slot(recv_count))
        copy = link(
            inv_ref.at[:, pl.ds(pl.multiple_of(lane * w, w), w)], head.at[0:2, rows_of(c, lane)],
            r, lax.rem(c + d, n_rhs), recv=inv_recv[-1],
        )
        copy.start()
        inv_copies.append(copy)

    lower_recv = [slot(recv_count) for _ in range(n_rhs)]
    lower_copies = []
    for source in range(n_rhs):
        sends = []
        for other in range(LANES):
            for side in range(n_rhs):
                if (other, side) != (1, source):
                    sends.append(link(
                        panel_ref.at[0, pl.ds(other * w, w)],
                        head.at[2, pl.ds(source * q + other * w, w)],
                        other, side, recv=lower_recv[source],
                    ))
        lower_copies.append(sends)

        @pl.when(is_second & (c == source))
        def _():
            for copy in sends:
                copy.start()

    step = q // PIECES
    tile_copies = []
    tile_recv = []
    for piece in range(PIECES):
        for d in range(1, n_rhs):
            tile_recv.append(slot(recv_count))
            tile_copies.append(link(
                panel_ref.at[:, pl.ds(piece * step, step)],
                tiles.at[:, pl.ds(pl.multiple_of(c * q + piece * step, step), step)],
                r, lax.rem(c + d, n_rhs), recv=tile_recv[-1],
            ))

    @pl.when(updates)
    def _():
        for copy in tile_copies:
            copy.start()

    px = pred_ref[0:1, :].astype(jnp.float32)
    py = pred_ref[1:2, :].astype(jnp.float32)
    pick = lax.broadcasted_iota(jnp.int32, (8, bs), 0) == 0
    strip = 32

    def cover(points, store, low, high):
        ox = jnp.broadcast_to(points[0], (8, bs)).astype(jnp.float32)
        oy = jnp.broadcast_to(points[1], (8, bs)).astype(jnp.float32)
        columns[...] = jnp.where(pick, ox, oy).T

        @pl.loop(low, high)
        def _(i):
            at = pl.ds(pl.multiple_of(i * strip, strip), strip)
            store(at, covariance(px, py, columns[at, 0:1], columns[at, 1:2]))

    def put_base(at, value):
        base[at, :] = value

    def put_first(at, value):
        first_rhs[at, :] = value.astype(jnp.bfloat16)

    def put_second(at, value):
        second_base[at, :] = value

    strips = bs // strip
    forwards = []

    def forward(src, row, recv):
        copy = link(src, src, row, c, recv=recv)
        forwards.append(copy)
        return copy

    def arrived(dst, recv):
        link(dst, dst, r, lax.rem(c + 1, n_rhs), send=0, recv=recv).wait_recv()

    chain_copies = []

    def along_chain(src, recv):
        copy = link(src, src, r + LANES, c, recv=recv)
        chain_copies.append(copy)

        @pl.when(has_next)
        def _():
            copy.start()

    for block in range(2):
        @pl.when(r != block)
        def _():
            arrived(lead_pts.at[block], point_recv[block])

        @pl.when(r == block)
        def _():
            copy = pltpu.make_async_copy(obs_ref, lead_pts.at[block], local_sem.at[3])
            copy.start()
            copy.wait()

        along_chain(lead_pts.at[block], point_recv[block])

    @pl.when(updates)
    def _():
        cover(obs_ref, put_base, 0, strips // 2)

    inv_from = [lax.rem(c + n_rhs - d, n_rhs) for d in range(1, n_rhs)]
    inv_x = [slot(recv_count) for _ in inv_from]
    inv_c = [slot(recv_count) for _ in inv_from]
    inv_xc = [slot(recv_count) for _ in inv_from]
    for k, side in enumerate(inv_from):
        part = head.at[0:2, rows_of(side, lane)]
        arrived(part, inv_recv[k])
        forward(part, x_side, inv_x[k]).start()
        forward(part, c_side, inv_c[k]).start()

    lower_x = [slot(recv_count) for _ in range(n_rhs)]
    lower_c = [slot(recv_count) for _ in range(n_rhs)]
    lower_xc = [slot(recv_count) for _ in range(n_rhs)]
    for side in range(n_rhs):
        part = head.at[2, rows_of(side, lane)]
        here = is_second & (c == side)

        @pl.when(jnp.logical_not(here))
        def _():
            arrived(part, lower_recv[side])

        @pl.when(here)
        def _():
            copy_lower.wait()

        along_chain(part, lower_recv[side])
        forward(part, x_side, lower_x[side]).start()
        forward(part, c_side, lower_c[side]).start()

    cover(lead_pts.at[0], put_first, 0, strips)

    for k, side in enumerate(inv_from):
        part = head.at[0:2, rows_of(side, x_lane)]
        arrived(part, inv_x[k])
        forward(part, c_side, inv_xc[k]).start()

    cover(lead_pts.at[1], put_second, 0, strips)

    for side in range(n_rhs):
        part = head.at[2, rows_of(side, x_lane)]
        arrived(part, lower_x[side])
        forward(part, c_side, lower_xc[side]).start()

    @pl.when(updates)
    def _():
        cover(obs_ref, put_base, strips // 2, strips)

    for k, side in enumerate(inv_from):
        arrived(head.at[0:2, rows_of(side, c_lane)], inv_c[k])
        arrived(head.at[0:2, rows_of(side, d_lane)], inv_xc[k])
    copy_inv.wait()

    half = solved.shape[2] // 2
    for n in range(2):
        at = slice(n * half, (n + 1) * half)
        solved[0, :, at] = jnp.dot(
            head[0], first_rhs[:, at], preferred_element_type=jnp.float32
        ).astype(jnp.bfloat16)

    for side in range(n_rhs):
        arrived(head.at[2, rows_of(side, c_lane)], lower_c[side])
        arrived(head.at[2, rows_of(side, d_lane)], lower_xc[side])

    for n in range(2):
        at = slice(n * half, (n + 1) * half)
        second_rhs = (second_base[:, at] - jnp.dot(
            head[2], solved[0, :, at], preferred_element_type=jnp.float32
        )).astype(jnp.bfloat16)
        solved[1, :, at] = jnp.dot(
            head[1], second_rhs, preferred_element_type=jnp.float32
        ).astype(jnp.bfloat16)

    copy_tiles.wait()

    def update(at, sem):
        total = base[at, :] - jnp.dot(tiles[0, at, :], solved[0], preferred_element_type=jnp.float32)
        total = total - jnp.dot(tiles[1, at, :], solved[1], preferred_element_type=jnp.float32)
        result[at, :] = total.astype(jnp.bfloat16)
        copy = pltpu.make_async_copy(result.at[at], out_ref.at[0, at], local_sem.at[sem])
        copy.start()
        return copy

    for block in range(2):
        @pl.when(r == block)
        def _():
            copy = pltpu.make_async_copy(solved.at[block], out_ref.at[0], local_sem.at[4])
            copy.start()
            copy.wait()

    @pl.when(updates)
    def _():
        writes = [update(own, 4)]
        sem = 5
        count = 0
        for piece in range(PIECES):
            for d in range(1, n_rhs):
                side = lax.rem(c + n_rhs - d, n_rhs)
                at = pl.ds(pl.multiple_of(side * q + piece * step, step), step)
                arrived(tiles.at[:, at], tile_recv[count])
                writes.append(update(at, sem))
                count += 1
                sem += 1
        for copy in writes:
            copy.wait()
        for copy in tile_copies:
            copy.wait_send()

    for block in range(2):
        @pl.when(r == block)
        def _():
            for copy in point_copies[block]:
                copy.wait_send()
    for copy in inv_copies + forwards:
        copy.wait_send()
    for source in range(n_rhs):
        @pl.when(is_second & (c == source))
        def _():
            for copy in lower_copies[source]:
                copy.wait_send()

    @pl.when(has_next)
    def _():
        for copy in chain_copies:
            copy.wait_send()


def on_device(n_rows, n_rhs, obs_points, pred_points, factor_panels, diag_inverse):
    panels = jnp.transpose(factor_panels[0], (1, 0, 2))
    bs = obs_points.shape[2]
    cols = pred_points.shape[1]
    bf16, f32 = jnp.bfloat16, jnp.float32
    copies = 64 + 24 * n_rhs * n_rhs
    return pl.pallas_call(
        functools.partial(kernel, n_rows, n_rhs),
        out_shape=jax.ShapeDtypeStruct((1, bs, cols), bf16),
        in_specs=[
            pl.BlockSpec(memory_space=pltpu.VMEM),
            pl.BlockSpec(memory_space=pltpu.VMEM),
            pl.BlockSpec(memory_space=pl.ANY),
            pl.BlockSpec(memory_space=pl.ANY),
        ],
        out_specs=pl.BlockSpec(memory_space=pl.ANY),
        scratch_shapes=[
            pltpu.VMEM((3, bs, bs), bf16),
            pltpu.VMEM((2, bs, bs), bf16),
            pltpu.VMEM((2, bs, cols), bf16),
            pltpu.VMEM((bs, cols), f32),
            pltpu.VMEM((bs, cols), bf16),
            pltpu.VMEM((bs, cols), f32),
            pltpu.VMEM((2,) + obs_points.shape, jnp.int32),
            pltpu.VMEM((bs, 8), f32),
            pltpu.VMEM((bs, cols), bf16),
            pltpu.SemaphoreType.DMA((8 + PIECES * n_rhs,)),
            pltpu.SemaphoreType.DMA((copies,)),
            pltpu.SemaphoreType.DMA((copies,)),
        ],
        compiler_params=pltpu.CompilerParams(
            collective_id=0, has_side_effects=True, vmem_limit_bytes=40 * 1024 * 1024
        ),
        cost_estimate=pl.CostEstimate(
            flops=10 * bs * bs * cols, bytes_accessed=4 * bs * cols, transcendentals=6 * bs * cols
        ),
    )(obs_points, pred_points, panels, diag_inverse)


def solution(mesh):
    in_specs = (
        P(None, None, "rows"),
        P(None, "rhs"),
        P(None, ("rows", "rhs"), None, None),
        P(None, "rhs", None),
    )
    body = functools.partial(on_device, mesh.shape["rows"], mesh.shape["rhs"])
    return jax.shard_map(
        body, mesh=mesh, in_specs=in_specs, out_specs=P(None, "rows", "rhs"), check_vma=False
    )
```

```python
import functools
import math

import jax
import jax.numpy as jnp
from jax import lax
from jax.experimental import pallas as pl
from jax.experimental.pallas import tpu as pltpu
from jax.sharding import PartitionSpec as P

SCALE = 16
SILL = 8.0
LANES = 4
PIECES = 2
RATE = math.sqrt(3.0) / SCALE * math.log2(math.e)
SLOPE = SILL * math.log(2.0)
MESH = pl.DeviceIdType.MESH


def covariance(px, py, ox, oy):
    dx = ox - px
    dy = oy - py
    square = dx * dx + dy * dy
    scaled = (square * RATE) * lax.rsqrt(jnp.maximum(square, 1e-6))
    return (SILL + SLOPE * scaled) * jnp.exp2(-scaled)


def kernel(
    n_rows, n_rhs, obs_ref, pred_ref, panel_ref, inv_ref, out_ref,
    head, tiles, solved, base, first_rhs, second_base, lead_pts, columns, result,
    local_sem, send_sem, recv_sem, spread_sem, point_sem,
):
    r = lax.axis_index("rows")
    c = lax.axis_index("rhs")
    bs = head.shape[1]
    q = bs // n_rhs
    w = q // LANES
    lane = lax.rem(r, LANES)
    x_side = r + 2 - 4 * (lane // 2)
    c_side = r + 1 - 2 * lax.rem(lane, 2)
    x_lane = lax.rem(x_side, LANES)
    c_lane = lax.rem(c_side, LANES)
    d_lane = lax.rem(c_lane + 2, LANES)
    is_first = r == 0
    is_second = r == 1
    updates = r >= 2

    send_count = [0]
    recv_count = [0]

    def slot(count):
        count[0] += 1
        return count[0] - 1

    def link(src, dst, row, side, send=None, recv=None):
        return pltpu.make_async_remote_copy(
            src_ref=src, dst_ref=dst,
            send_sem=send_sem.at[slot(send_count) if send is None else send],
            recv_sem=recv_sem.at[slot(recv_count) if recv is None else recv],
            device_id=(row, side), device_id_type=MESH,
        )

    def rows_of(side, which):
        return pl.ds(pl.multiple_of(side * q + which * w, w), w)

    def chunk(side):
        return pl.ds(pl.multiple_of(side * q, q), q)

    own = chunk(c)
    copy_inv = pltpu.make_async_copy(inv_ref, head.at[0:2, own], local_sem.at[0])
    copy_tiles = pltpu.make_async_copy(panel_ref, tiles.at[:, own], local_sem.at[1])
    copy_lower = pltpu.make_async_copy(
        panel_ref.at[0, pl.ds(w, w)], head.at[2, rows_of(c, 1)], local_sem.at[2]
    )
    copy_inv.start()
    copy_tiles.start()

    @pl.when(is_second)
    def _():
        copy_lower.start()

    barrier = pltpu.get_barrier_semaphore()

    def greet(row, side):
        pl.semaphore_signal(barrier, inc=1, device_id=(row, side), device_id_type=MESH)

    for d in range(1, n_rhs):
        greet(r, lax.rem(c + d, n_rhs))
    greet(x_side, c)
    greet(c_side, c)

    @pl.when(r != 0)
    def _():
        greet(0, c)

    for side in range(n_rhs):
        @pl.when(jnp.logical_not(is_second & (c == side)))
        def _():
            greet(1, side)

    pl.semaphore_wait(
        barrier,
        n_rhs + 1
        + is_first.astype(jnp.int32) * (n_rows - 1)
        + is_second.astype(jnp.int32) * (n_rows * n_rhs - 1),
    )

    inv_copies = []
    inv_recv = []
    for k in range(2):
        for d in range(1, n_rhs):
            inv_recv.append(slot(recv_count))
            copy = link(
                inv_ref.at[k, pl.ds(pl.multiple_of(lane * w, w), w)], head.at[k, rows_of(c, lane)],
                r, lax.rem(c + d, n_rhs), recv=inv_recv[-1],
            )
            copy.start()
            inv_copies.append(copy)

    point_recv = [slot(recv_count) for _ in range(2)]

    def point_copy(block, row):
        return pltpu.make_async_remote_copy(
            src_ref=obs_ref, dst_ref=lead_pts.at[block], send_sem=point_sem.at[row],
            recv_sem=recv_sem.at[point_recv[block]], device_id=(row, c), device_id_type=MESH,
        )

    def each_point(block, act):
        @pl.when(r == block)
        def _():
            @pl.loop(0, n_rows)
            def _(row):
                @pl.when(row != block)
                def _():
                    act(point_copy(block, row))

    for block in range(2):
        each_point(block, lambda copy: copy.start())

    lower_recv = [slot(recv_count) for _ in range(n_rhs)]

    def lower_copy(source, row, side):
        which = lax.rem(row, LANES)
        return pltpu.make_async_remote_copy(
            src_ref=panel_ref.at[0, pl.ds(pl.multiple_of(which * w, w), w)],
            dst_ref=head.at[2, rows_of(source, which)],
            send_sem=spread_sem.at[row * n_rhs + side],
            recv_sem=recv_sem.at[lower_recv[source]],
            device_id=(row, side), device_id_type=MESH,
        )

    def each_lower(act):
        for source in range(n_rhs):
            @pl.when(is_second & (c == source))
            def _():
                @pl.loop(0, n_rows)
                def _(back):
                    row = n_rows - 1 - back
                    for side in range(n_rhs):
                        if side == source:
                            @pl.when(row != 1)
                            def _():
                                act(lower_copy(source, row, side))
                        else:
                            act(lower_copy(source, row, side))

    each_lower(lambda copy: copy.start())

    step = q // PIECES
    tile_copies = []
    tile_recv = []
    for piece in range(PIECES):
        for d in range(1, n_rhs):
            tile_recv.append(slot(recv_count))
            tile_copies.append(link(
                panel_ref.at[:, pl.ds(piece * step, step)],
                tiles.at[:, pl.ds(pl.multiple_of(c * q + piece * step, step), step)],
                r, lax.rem(c + d, n_rhs), recv=tile_recv[-1],
            ))

    @pl.when(updates)
    def _():
        for copy in tile_copies:
            copy.start()

    px = pred_ref[0:1, :].astype(jnp.float32)
    py = pred_ref[1:2, :].astype(jnp.float32)
    pick = lax.broadcasted_iota(jnp.int32, (8, bs), 0) == 0
    strip = 32

    def cover(points, store, low, high):
        ox = jnp.broadcast_to(points[0], (8, bs)).astype(jnp.float32)
        oy = jnp.broadcast_to(points[1], (8, bs)).astype(jnp.float32)
        columns[...] = jnp.where(pick, ox, oy).T

        @pl.loop(low, high)
        def _(i):
            at = pl.ds(pl.multiple_of(i * strip, strip), strip)
            store(at, covariance(px, py, columns[at, 0:1], columns[at, 1:2]))

    def put_base(at, value):
        base[at, :] = value

    def put_first(at, value):
        first_rhs[at, :] = value.astype(jnp.bfloat16)

    def put_second(at, value):
        second_base[at, :] = value

    strips = bs // strip
    forwards = []

    def forward(src, row, recv):
        copy = link(src, src, row, c, recv=recv)
        forwards.append(copy)
        return copy

    def arrived(dst, recv):
        link(dst, dst, r, lax.rem(c + 1, n_rhs), send=0, recv=recv).wait_recv()

    @pl.when(updates)
    def _():
        cover(obs_ref, put_base, 0, strips // 2)

    inv_from = [
        (k, lax.rem(c + n_rhs - d, n_rhs)) for k in range(2) for d in range(1, n_rhs)
    ]
    inv_x = [slot(recv_count) for _ in inv_from]
    inv_c = [slot(recv_count) for _ in inv_from]
    inv_xc = [slot(recv_count) for _ in inv_from]
    for n, (k, side) in enumerate(inv_from):
        part = head.at[k, rows_of(side, lane)]
        arrived(part, inv_recv[n])
        forward(part, x_side, inv_x[n]).start()
        forward(part, c_side, inv_c[n]).start()

    for block in range(2):
        @pl.when(r != block)
        def _():
            arrived(lead_pts.at[block], point_recv[block])

        @pl.when(r == block)
        def _():
            copy = pltpu.make_async_copy(obs_ref, lead_pts.at[block], local_sem.at[3])
            copy.start()
            copy.wait()

    cover(lead_pts.at[0], put_first, 0, strips)

    for n, (k, side) in enumerate(inv_from):
        part = head.at[k, rows_of(side, x_lane)]
        arrived(part, inv_x[n])
        forward(part, c_side, inv_xc[n]).start()

    lower_x = [slot(recv_count) for _ in range(n_rhs)]
    lower_c = [slot(recv_count) for _ in range(n_rhs)]
    lower_xc = [slot(recv_count) for _ in range(n_rhs)]
    for side in range(n_rhs):
        part = head.at[2, rows_of(side, lane)]
        here = is_second & (c == side)

        @pl.when(jnp.logical_not(here))
        def _():
            arrived(part, lower_recv[side])

        @pl.when(here)
        def _():
            copy_lower.wait()

        forward(part, x_side, lower_x[side]).start()
        forward(part, c_side, lower_c[side]).start()

    cover(lead_pts.at[1], put_second, 0, strips)

    for side in range(n_rhs):
        part = head.at[2, rows_of(side, x_lane)]
        arrived(part, lower_x[side])
        forward(part, c_side, lower_xc[side]).start()

    @pl.when(updates)
    def _():
        cover(obs_ref, put_base, strips // 2, strips)

    copy_inv.wait()

    def inverse_here(block):
        for n, (k, side) in enumerate(inv_from):
            if k == block:
                arrived(head.at[k, rows_of(side, c_lane)], inv_c[n])
                arrived(head.at[k, rows_of(side, d_lane)], inv_xc[n])

    inverse_here(0)
    half = solved.shape[2] // 2
    for n in range(2):
        at = slice(n * half, (n + 1) * half)
        solved[0, :, at] = jnp.dot(
            head[0], first_rhs[:, at], preferred_element_type=jnp.float32
        ).astype(jnp.bfloat16)

    for side in range(n_rhs):
        arrived(head.at[2, rows_of(side, c_lane)], lower_c[side])
        arrived(head.at[2, rows_of(side, d_lane)], lower_xc[side])
    inverse_here(1)

    for n in range(2):
        at = slice(n * half, (n + 1) * half)
        second_rhs = (second_base[:, at] - jnp.dot(
            head[2], solved[0, :, at], preferred_element_type=jnp.float32
        )).astype(jnp.bfloat16)
        solved[1, :, at] = jnp.dot(
            head[1], second_rhs, preferred_element_type=jnp.float32
        ).astype(jnp.bfloat16)

    copy_tiles.wait()

    def update(at, sem):
        total = base[at, :] - jnp.dot(tiles[0, at, :], solved[0], preferred_element_type=jnp.float32)
        total = total - jnp.dot(tiles[1, at, :], solved[1], preferred_element_type=jnp.float32)
        result[at, :] = total.astype(jnp.bfloat16)
        copy = pltpu.make_async_copy(result.at[at], out_ref.at[0, at], local_sem.at[sem])
        copy.start()
        return copy

    for block in range(2):
        @pl.when(r == block)
        def _():
            copy = pltpu.make_async_copy(solved.at[block], out_ref.at[0], local_sem.at[4])
            copy.start()
            copy.wait()

    @pl.when(updates)
    def _():
        writes = [update(own, 4)]
        sem = 5
        count = 0
        for piece in range(PIECES):
            for d in range(1, n_rhs):
                side = lax.rem(c + n_rhs - d, n_rhs)
                at = pl.ds(pl.multiple_of(side * q + piece * step, step), step)
                arrived(tiles.at[:, at], tile_recv[count])
                writes.append(update(at, sem))
                count += 1
                sem += 1
        for copy in writes:
            copy.wait()
        for copy in tile_copies:
            copy.wait_send()

    for block in range(2):
        each_point(block, lambda copy: copy.wait_send())
    for copy in inv_copies + forwards:
        copy.wait_send()
    each_lower(lambda copy: copy.wait_send())


def on_device(n_rows, n_rhs, obs_points, pred_points, factor_panels, diag_inverse):
    panels = jnp.transpose(factor_panels[0], (1, 0, 2))
    bs = obs_points.shape[2]
    cols = pred_points.shape[1]
    bf16, f32 = jnp.bfloat16, jnp.float32
    copies = 16 + 20 * n_rhs
    return pl.pallas_call(
        functools.partial(kernel, n_rows, n_rhs),
        out_shape=jax.ShapeDtypeStruct((1, bs, cols), bf16),
        in_specs=[
            pl.BlockSpec(memory_space=pltpu.VMEM),
            pl.BlockSpec(memory_space=pltpu.VMEM),
            pl.BlockSpec(memory_space=pl.ANY),
            pl.BlockSpec(memory_space=pl.ANY),
        ],
        out_specs=pl.BlockSpec(memory_space=pl.ANY),
        scratch_shapes=[
            pltpu.VMEM((3, bs, bs), bf16),
            pltpu.VMEM((2, bs, bs), bf16),
            pltpu.VMEM((2, bs, cols), bf16),
            pltpu.VMEM((bs, cols), f32),
            pltpu.VMEM((bs, cols), bf16),
            pltpu.VMEM((bs, cols), f32),
            pltpu.VMEM((2,) + obs_points.shape, jnp.int32),
            pltpu.VMEM((bs, 8), f32),
            pltpu.VMEM((bs, cols), bf16),
            pltpu.SemaphoreType.DMA((8 + PIECES * n_rhs,)),
            pltpu.SemaphoreType.DMA((copies,)),
            pltpu.SemaphoreType.DMA((copies,)),
            pltpu.SemaphoreType.DMA((n_rows * n_rhs,)),
            pltpu.SemaphoreType.DMA((n_rows,)),
        ],
        compiler_params=pltpu.CompilerParams(
            collective_id=0, has_side_effects=True, vmem_limit_bytes=40 * 1024 * 1024
        ),
        cost_estimate=pl.CostEstimate(
            flops=10 * bs * bs * cols, bytes_accessed=4 * bs * cols, transcendentals=6 * bs * cols
        ),
    )(obs_points, pred_points, panels, diag_inverse)


def solution(mesh):
    in_specs = (
        P(None, None, "rows"),
        P(None, "rhs"),
        P(None, ("rows", "rhs"), None, None),
        P(None, "rhs", None),
    )
    body = functools.partial(on_device, mesh.shape["rows"], mesh.shape["rhs"])
    return jax.shard_map(
        body, mesh=mesh, in_specs=in_specs, out_specs=P(None, "rows", "rhs"), check_vma=False
    )
```

```python
import functools
import math

import jax
import jax.numpy as jnp
from jax import lax
from jax.experimental import pallas as pl
from jax.experimental.pallas import tpu as pltpu
from jax.sharding import PartitionSpec as P

SCALE = 16
SILL = 8.0
LANES = 4
PIECES = 2
RATE = math.sqrt(3.0) / SCALE * math.log2(math.e)
SLOPE = SILL * math.log(2.0)
MESH = pl.DeviceIdType.MESH


def covariance(px, py, ox, oy):
    dx = ox - px
    dy = oy - py
    square = dx * dx + dy * dy
    scaled = (square * RATE) * lax.rsqrt(jnp.maximum(square, 1e-6))
    return (SILL + SLOPE * scaled) * jnp.exp2(-scaled)


def kernel(
    n_rows, n_rhs, obs_ref, pred_ref, panel_ref, inv_ref, out_ref,
    head, tiles, solved, base, first_rhs, second_base, lead_pts, columns, result,
    local_sem, send_sem, recv_sem,
):
    r = lax.axis_index("rows")
    c = lax.axis_index("rhs")
    bs = head.shape[1]
    q = bs // n_rhs
    w = q // LANES
    lane = lax.rem(r, LANES)
    hop = r // LANES
    hops = n_rows // LANES
    has_next = hop < hops - 1
    has_prev = hop > 0
    x_side = r + 2 - 4 * (lane // 2)
    c_side = r + 1 - 2 * lax.rem(lane, 2)
    x_lane = lax.rem(x_side, LANES)
    c_lane = lax.rem(c_side, LANES)
    d_lane = lax.rem(c_lane + 2, LANES)
    is_first = r == 0
    is_second = r == 1
    updates = r >= 2

    send_count = [0]
    recv_count = [0]

    def slot(count):
        count[0] += 1
        return count[0] - 1

    def link(src, dst, row, side, send=None, recv=None):
        return pltpu.make_async_remote_copy(
            src_ref=src, dst_ref=dst,
            send_sem=send_sem.at[slot(send_count) if send is None else send],
            recv_sem=recv_sem.at[slot(recv_count) if recv is None else recv],
            device_id=(row, side), device_id_type=MESH,
        )

    def rows_of(side, which):
        return pl.ds(pl.multiple_of(side * q + which * w, w), w)

    def chunk(side):
        return pl.ds(pl.multiple_of(side * q, q), q)

    own = chunk(c)
    copy_inv = pltpu.make_async_copy(inv_ref, head.at[0:2, own], local_sem.at[0])
    copy_tiles = pltpu.make_async_copy(panel_ref, tiles.at[:, own], local_sem.at[1])
    copy_lower = pltpu.make_async_copy(
        panel_ref.at[0, pl.ds(w, w)], head.at[2, rows_of(c, 1)], local_sem.at[2]
    )
    copy_inv.start()
    copy_tiles.start()

    @pl.when(is_second)
    def _():
        copy_lower.start()

    barrier = pltpu.get_barrier_semaphore()

    def greet(row, side):
        pl.semaphore_signal(barrier, inc=1, device_id=(row, side), device_id_type=MESH)

    for d in range(1, n_rhs):
        greet(r, lax.rem(c + d, n_rhs))
    mates = [hop * LANES + lax.rem(lane + d, LANES) for d in range(1, LANES)]
    for mate in mates:
        greet(mate, c)
    passes_points = lane < 2

    @pl.when(has_prev)
    def _():
        greet(r - LANES, c)

    @pl.when(has_prev & passes_points)
    def _():
        greet(lane, c)

    @pl.when(hop == 0)
    def _():
        for d in range(1, n_rhs):
            greet(1, lax.rem(c + d, n_rhs))

    pl.semaphore_wait(
        barrier,
        n_rhs + LANES - 2
        + has_next.astype(jnp.int32)
        + (r < 2).astype(jnp.int32) * (hops - 1)
        + is_second.astype(jnp.int32) * (LANES * (n_rhs - 1)),
    )

    inv_copies = []
    inv_recv = []
    for k in range(2):
        for d in range(1, n_rhs):
            inv_recv.append(slot(recv_count))
            copy = link(
                inv_ref.at[k, pl.ds(pl.multiple_of(lane * w, w), w)], head.at[k, rows_of(c, lane)],
                r, lax.rem(c + d, n_rhs), recv=inv_recv[-1],
            )
            copy.start()
            inv_copies.append(copy)

    point_recv = [slot(recv_count) for _ in range(2)]
    far_copies = []
    for block in range(2):
        sends = [
            link(obs_ref, lead_pts.at[block], block + LANES * h, c, recv=point_recv[block])
            for h in range(1, hops)
        ]
        far_copies.append(sends)

        @pl.when(r == block)
        def _():
            for copy in sends:
                copy.start()
    mate_copies = [
        [link(lead_pts.at[block], lead_pts.at[block], mate, c, recv=point_recv[block]) for mate in mates]
        for block in range(2)
    ]

    lower_recv = [slot(recv_count) for _ in range(n_rhs)]
    lower_copies = []
    for source in range(n_rhs):
        sends = []
        for other in range(LANES):
            for side in range(n_rhs):
                if (other, side) != (1, source):
                    sends.append(link(
                        panel_ref.at[0, pl.ds(other * w, w)],
                        head.at[2, pl.ds(source * q + other * w, w)],
                        other, side, recv=lower_recv[source],
                    ))
        lower_copies.append(sends)

        @pl.when(is_second & (c == source))
        def _():
            for copy in sends:
                copy.start()

    step = q // PIECES
    tile_copies = []
    tile_recv = []
    for piece in range(PIECES):
        for d in range(1, n_rhs):
            tile_recv.append(slot(recv_count))
            tile_copies.append(link(
                panel_ref.at[:, pl.ds(piece * step, step)],
                tiles.at[:, pl.ds(pl.multiple_of(c * q + piece * step, step), step)],
                r, lax.rem(c + d, n_rhs), recv=tile_recv[-1],
            ))

    @pl.when(updates)
    def _():
        for copy in tile_copies:
            copy.start()

    px = pred_ref[0:1, :].astype(jnp.float32)
    py = pred_ref[1:2, :].astype(jnp.float32)
    strip = 32
    width = 2 * bs // 8
    groups = bs // width

    def cover(points, store, low, high):
        columns[...] = points[...].astype(jnp.float32).T
        for g in range(low, high):
            @pl.loop(0, width // strip)
            def _(i):
                part = pl.ds(pl.multiple_of(i * strip, strip), strip)
                at = pl.ds(pl.multiple_of(g * width + i * strip, strip), strip)
                ox = columns[part, g:g + 1]
                oy = columns[part, groups + g:groups + g + 1]
                store(at, covariance(px, py, ox, oy))

    def put_base(at, value):
        base[at, :] = value

    def put_first(at, value):
        first_rhs[at, :] = value.astype(jnp.bfloat16)

    def put_second(at, value):
        second_base[at, :] = value

    forwards = []

    def forward(src, row, recv):
        copy = link(src, src, row, c, recv=recv)
        forwards.append(copy)
        return copy

    def arrived(dst, recv):
        link(dst, dst, r, lax.rem(c + 1, n_rhs), send=0, recv=recv).wait_recv()

    def points_here(block):
        @pl.when(r == block)
        def _():
            copy = pltpu.make_async_copy(obs_ref, lead_pts.at[block], local_sem.at[3])
            copy.start()
            copy.wait()

        @pl.when(r != block)
        def _():
            arrived(lead_pts.at[block], point_recv[block])

        @pl.when(lane == block)
        def _():
            for copy in mate_copies[block]:
                copy.start()

    lower_send = [[slot(send_count) for _ in range(3)] for _ in range(n_rhs)]
    lower_x = [slot(recv_count) for _ in range(n_rhs)]
    lower_c = [slot(recv_count) for _ in range(n_rhs)]
    lower_xc = [slot(recv_count) for _ in range(n_rhs)]

    def lower_links(side):
        part = head.at[2, rows_of(side, lane)]
        sends = lower_send[side]
        return (
            link(part, part, r + LANES, c, send=sends[0], recv=lower_recv[side]),
            link(part, part, x_side, c, send=sends[1], recv=lower_x[side]),
            link(part, part, c_side, c, send=sends[2], recv=lower_c[side]),
        )

    def lower_step(turn):
        @pl.when(turn)
        def _():
            for side in range(n_rhs):
                part = head.at[2, rows_of(side, lane)]
                here = is_second & (c == side)

                @pl.when(jnp.logical_not(here))
                def _():
                    arrived(part, lower_recv[side])

                @pl.when(here)
                def _():
                    copy_lower.wait()

                on, across, beside = lower_links(side)

                @pl.when(has_next)
                def _():
                    on.start()

                across.start()
                beside.start()

    @pl.when(passes_points)
    def _():
        for block in range(2):
            @pl.when(lane == block)
            def _():
                points_here(block)
    lower_step(hop == 0)

    @pl.when(updates)
    def _():
        cover(obs_ref, put_base, 0, groups // 2)

    inv_from = [
        (k, lax.rem(c + n_rhs - d, n_rhs)) for k in range(2) for d in range(1, n_rhs)
    ]
    inv_x = [slot(recv_count) for _ in inv_from]
    inv_c = [slot(recv_count) for _ in inv_from]
    inv_xc = [slot(recv_count) for _ in inv_from]
    for n, (k, side) in enumerate(inv_from):
        part = head.at[k, rows_of(side, lane)]
        arrived(part, inv_recv[n])
        forward(part, x_side, inv_x[n]).start()
        forward(part, c_side, inv_c[n]).start()
    lower_step(hop == 1)

    for block in range(2):
        @pl.when(lane != block)
        def _():
            arrived(lead_pts.at[block], point_recv[block])

    cover(lead_pts.at[0], put_first, 0, groups)

    for n, (k, side) in enumerate(inv_from):
        part = head.at[k, rows_of(side, x_lane)]
        arrived(part, inv_x[n])
        forward(part, c_side, inv_xc[n]).start()
    lower_step(hop == 2)

    cover(lead_pts.at[1], put_second, 0, groups)
    lower_step(hop >= 3)

    copy_inv.wait()

    def inverse_here(block):
        for n, (k, side) in enumerate(inv_from):
            if k == block:
                arrived(head.at[k, rows_of(side, c_lane)], inv_c[n])
                arrived(head.at[k, rows_of(side, d_lane)], inv_xc[n])

    inverse_here(0)
    half = solved.shape[2] // 2
    for n in range(2):
        at = slice(n * half, (n + 1) * half)
        solved[0, :, at] = jnp.dot(
            head[0], first_rhs[:, at], preferred_element_type=jnp.float32
        ).astype(jnp.bfloat16)

    for side in range(n_rhs):
        part = head.at[2, rows_of(side, x_lane)]
        arrived(part, lower_x[side])
        forward(part, c_side, lower_xc[side]).start()

    @pl.when(updates)
    def _():
        cover(obs_ref, put_base, groups // 2, groups)

    for side in range(n_rhs):
        arrived(head.at[2, rows_of(side, c_lane)], lower_c[side])
        arrived(head.at[2, rows_of(side, d_lane)], lower_xc[side])
    inverse_here(1)

    for n in range(2):
        at = slice(n * half, (n + 1) * half)
        second_rhs = (second_base[:, at] - jnp.dot(
            head[2], solved[0, :, at], preferred_element_type=jnp.float32
        )).astype(jnp.bfloat16)
        solved[1, :, at] = jnp.dot(
            head[1], second_rhs, preferred_element_type=jnp.float32
        ).astype(jnp.bfloat16)

    copy_tiles.wait()

    def update(at, sem):
        total = base[at, :] - jnp.dot(tiles[0, at, :], solved[0], preferred_element_type=jnp.float32)
        total = total - jnp.dot(tiles[1, at, :], solved[1], preferred_element_type=jnp.float32)
        result[at, :] = total.astype(jnp.bfloat16)
        copy = pltpu.make_async_copy(result.at[at], out_ref.at[0, at], local_sem.at[sem])
        copy.start()
        return copy

    for block in range(2):
        @pl.when(r == block)
        def _():
            copy = pltpu.make_async_copy(solved.at[block], out_ref.at[0], local_sem.at[4])
            copy.start()
            copy.wait()

    @pl.when(updates)
    def _():
        writes = [update(own, 4)]
        sem = 5
        count = 0
        for piece in range(PIECES):
            for d in range(1, n_rhs):
                side = lax.rem(c + n_rhs - d, n_rhs)
                at = pl.ds(pl.multiple_of(side * q + piece * step, step), step)
                arrived(tiles.at[:, at], tile_recv[count])
                writes.append(update(at, sem))
                count += 1
                sem += 1
        for copy in writes:
            copy.wait()
        for copy in tile_copies:
            copy.wait_send()

    for block in range(2):
        @pl.when(r == block)
        def _():
            for copy in far_copies[block]:
                copy.wait_send()

        @pl.when(lane == block)
        def _():
            for copy in mate_copies[block]:
                copy.wait_send()
    for copy in inv_copies + forwards:
        copy.wait_send()
    for source in range(n_rhs):
        @pl.when(is_second & (c == source))
        def _():
            for copy in lower_copies[source]:
                copy.wait_send()
    for side in range(n_rhs):
        on, across, beside = lower_links(side)

        @pl.when(has_next)
        def _():
            on.wait_send()

        across.wait_send()
        beside.wait_send()


def on_device(n_rows, n_rhs, obs_points, pred_points, factor_panels, diag_inverse):
    panels = jnp.transpose(factor_panels[0], (1, 0, 2))
    bs = obs_points.shape[2]
    cols = pred_points.shape[1]
    bf16, f32 = jnp.bfloat16, jnp.float32
    copies = 32 + 2 * n_rows + 16 * n_rhs + LANES * n_rhs * n_rhs
    return pl.pallas_call(
        functools.partial(kernel, n_rows, n_rhs),
        out_shape=jax.ShapeDtypeStruct((1, bs, cols), bf16),
        in_specs=[
            pl.BlockSpec(memory_space=pltpu.VMEM),
            pl.BlockSpec(memory_space=pltpu.VMEM),
            pl.BlockSpec(memory_space=pl.ANY),
            pl.BlockSpec(memory_space=pl.ANY),
        ],
        out_specs=pl.BlockSpec(memory_space=pl.ANY),
        scratch_shapes=[
            pltpu.VMEM((3, bs, bs), bf16),
            pltpu.VMEM((2, bs, bs), bf16),
            pltpu.VMEM((2, bs, cols), bf16),
            pltpu.VMEM((bs, cols), f32),
            pltpu.VMEM((bs, cols), bf16),
            pltpu.VMEM((bs, cols), f32),
            pltpu.VMEM((2, 8, 2 * bs // 8), jnp.int32),
            pltpu.VMEM((2 * bs // 8, 8), f32),
            pltpu.VMEM((bs, cols), bf16),
            pltpu.SemaphoreType.DMA((8 + PIECES * n_rhs,)),
            pltpu.SemaphoreType.DMA((copies,)),
            pltpu.SemaphoreType.DMA((copies,)),
        ],
        compiler_params=pltpu.CompilerParams(
            collective_id=0, has_side_effects=True, vmem_limit_bytes=40 * 1024 * 1024
        ),
        cost_estimate=pl.CostEstimate(
            flops=10 * bs * bs * cols, bytes_accessed=4 * bs * cols, transcendentals=6 * bs * cols
        ),
    )(obs_points.reshape(8, 2 * bs // 8), pred_points, panels, diag_inverse)


def solution(mesh):
    in_specs = (
        P(None, None, "rows"),
        P(None, "rhs"),
        P(None, ("rows", "rhs"), None, None),
        P(None, "rhs", None),
    )
    body = functools.partial(on_device, mesh.shape["rows"], mesh.shape["rhs"])
    return jax.shard_map(
        body, mesh=mesh, in_specs=in_specs, out_specs=P(None, "rows", "rhs"), check_vma=False
    )
```

```python
import functools
import math

import jax
import jax.numpy as jnp
from jax import lax
from jax.experimental import pallas as pl
from jax.experimental.pallas import tpu as pltpu
from jax.sharding import PartitionSpec as P

SCALE = 16
SILL = 8.0
LANES = 4
PIECES = 2
RATE = math.sqrt(3.0) / SCALE * math.log2(math.e)
SLOPE = SILL * math.log(2.0)
MESH = pl.DeviceIdType.MESH


def covariance(px, py, ox, oy):
    dx = ox - px
    dy = oy - py
    square = dx * dx + dy * dy
    scaled = (square * RATE) * lax.rsqrt(jnp.maximum(square, 1e-6))
    return (SILL + SLOPE * scaled) * jnp.exp2(-scaled)


def kernel(
    n_rows, n_rhs, obs_ref, pred_ref, panel_ref, inv_ref, out_ref,
    head, tiles, solved, base, first_rhs, second_base, lead_pts, columns, result,
    local_sem, send_sem, recv_sem,
):
    r = lax.axis_index("rows")
    c = lax.axis_index("rhs")
    bs = head.shape[1]
    q = bs // n_rhs
    w = q // LANES
    lane = lax.rem(r, LANES)
    hop = r // LANES
    hops = n_rows // LANES
    middle = (hops + 1) // 2
    depth = hop - middle * (hop >= middle).astype(jnp.int32) + (hop >= middle).astype(jnp.int32)
    has_next = (hop < hops - 1) & (hop + 1 != middle)
    has_prev = (hop > 0) & (hop != middle)
    x_side = r + 2 - 4 * (lane // 2)
    c_side = r + 1 - 2 * lax.rem(lane, 2)
    x_lane = lax.rem(x_side, LANES)
    c_lane = lax.rem(c_side, LANES)
    d_lane = lax.rem(c_lane + 2, LANES)
    is_first = r == 0
    is_second = r == 1
    updates = r >= 2

    send_count = [0]
    recv_count = [0]

    def slot(count):
        count[0] += 1
        return count[0] - 1

    def link(src, dst, row, side, send=None, recv=None):
        return pltpu.make_async_remote_copy(
            src_ref=src, dst_ref=dst,
            send_sem=send_sem.at[slot(send_count) if send is None else send],
            recv_sem=recv_sem.at[slot(recv_count) if recv is None else recv],
            device_id=(row, side), device_id_type=MESH,
        )

    def rows_of(side, which):
        return pl.ds(pl.multiple_of(side * q + which * w, w), w)

    def chunk(side):
        return pl.ds(pl.multiple_of(side * q, q), q)

    own = chunk(c)
    copy_inv = pltpu.make_async_copy(inv_ref, head.at[0:2, own], local_sem.at[0])
    copy_tiles = pltpu.make_async_copy(panel_ref, tiles.at[:, own], local_sem.at[1])
    copy_lower = pltpu.make_async_copy(
        panel_ref.at[0, pl.ds(w, w)], head.at[2, rows_of(c, 1)], local_sem.at[2]
    )
    copy_inv.start()
    copy_tiles.start()

    @pl.when(is_second)
    def _():
        copy_lower.start()

    barrier = pltpu.get_barrier_semaphore()

    def greet(row, side):
        pl.semaphore_signal(barrier, inc=1, device_id=(row, side), device_id_type=MESH)

    for d in range(1, n_rhs):
        greet(r, lax.rem(c + d, n_rhs))
    mates = [hop * LANES + lax.rem(lane + d, LANES) for d in range(1, LANES)]
    for mate in mates:
        greet(mate, c)
    passes_points = lane < 2

    @pl.when(has_prev)
    def _():
        greet(r - LANES, c)

    @pl.when((hop > 0) & passes_points)
    def _():
        greet(lane, c)

    @pl.when(hop == middle)
    def _():
        for side in range(n_rhs):
            greet(1, side)

    @pl.when(hop == 0)
    def _():
        for d in range(1, n_rhs):
            greet(1, lax.rem(c + d, n_rhs))

    pl.semaphore_wait(
        barrier,
        n_rhs + LANES - 2
        + has_next.astype(jnp.int32)
        + (r < 2).astype(jnp.int32) * (hops - 1)
        + is_second.astype(jnp.int32) * (LANES * (n_rhs - 1 + n_rhs)),
    )

    inv_copies = []
    inv_recv = []
    for k in range(2):
        for d in range(1, n_rhs):
            inv_recv.append(slot(recv_count))
            copy = link(
                inv_ref.at[k, pl.ds(pl.multiple_of(lane * w, w), w)], head.at[k, rows_of(c, lane)],
                r, lax.rem(c + d, n_rhs), recv=inv_recv[-1],
            )
            copy.start()
            inv_copies.append(copy)

    point_recv = [slot(recv_count) for _ in range(2)]
    far_copies = []
    for block in range(2):
        sends = [
            link(obs_ref, lead_pts.at[block], block + LANES * h, c, recv=point_recv[block])
            for h in range(1, hops)
        ]
        far_copies.append(sends)

        @pl.when(r == block)
        def _():
            for copy in sends:
                copy.start()
    mate_copies = [
        [link(lead_pts.at[block], lead_pts.at[block], mate, c, recv=point_recv[block]) for mate in mates]
        for block in range(2)
    ]

    lower_recv = [slot(recv_count) for _ in range(n_rhs)]
    lower_copies = []
    for source in range(n_rhs):
        sends = [
            link(
                panel_ref.at[0, pl.ds(other * w, w)],
                head.at[2, pl.ds(source * q + other * w, w)],
                middle * LANES + other, side, recv=lower_recv[source],
            )
            for other in range(LANES) for side in range(n_rhs)
        ]
        for other in range(LANES):
            for side in range(n_rhs):
                if (other, side) != (1, source):
                    sends.append(link(
                        panel_ref.at[0, pl.ds(other * w, w)],
                        head.at[2, pl.ds(source * q + other * w, w)],
                        other, side, recv=lower_recv[source],
                    ))
        lower_copies.append(sends)

        @pl.when(is_second & (c == source))
        def _():
            for copy in sends:
                copy.start()

    step = q // PIECES
    tile_copies = []
    tile_recv = []
    for piece in range(PIECES):
        for d in range(1, n_rhs):
            tile_recv.append(slot(recv_count))
            tile_copies.append(link(
                panel_ref.at[:, pl.ds(piece * step, step)],
                tiles.at[:, pl.ds(pl.multiple_of(c * q + piece * step, step), step)],
                r, lax.rem(c + d, n_rhs), recv=tile_recv[-1],
            ))

    @pl.when(updates)
    def _():
        for copy in tile_copies:
            copy.start()

    px = pred_ref[0:1, :].astype(jnp.float32)
    py = pred_ref[1:2, :].astype(jnp.float32)
    strip = 32
    width = 2 * bs // 8
    groups = bs // width

    def cover(points, store, low, high):
        columns[...] = points[...].astype(jnp.float32).T
        for g in range(low, high):
            @pl.loop(0, width // strip)
            def _(i):
                part = pl.ds(pl.multiple_of(i * strip, strip), strip)
                at = pl.ds(pl.multiple_of(g * width + i * strip, strip), strip)
                ox = columns[part, g:g + 1]
                oy = columns[part, groups + g:groups + g + 1]
                store(at, covariance(px, py, ox, oy))

    def put_base(at, value):
        base[at, :] = value

    def put_first(at, value):
        first_rhs[at, :] = value.astype(jnp.bfloat16)

    def put_second(at, value):
        second_base[at, :] = value

    forwards = []

    def forward(src, row, recv):
        copy = link(src, src, row, c, recv=recv)
        forwards.append(copy)
        return copy

    def arrived(dst, recv):
        link(dst, dst, r, lax.rem(c + 1, n_rhs), send=0, recv=recv).wait_recv()

    def points_here(block):
        @pl.when(r == block)
        def _():
            copy = pltpu.make_async_copy(obs_ref, lead_pts.at[block], local_sem.at[3])
            copy.start()
            copy.wait()

        @pl.when(r != block)
        def _():
            arrived(lead_pts.at[block], point_recv[block])

        @pl.when(lane == block)
        def _():
            for copy in mate_copies[block]:
                copy.start()

    lower_send = [[slot(send_count) for _ in range(3)] for _ in range(n_rhs)]
    lower_x = [slot(recv_count) for _ in range(n_rhs)]
    lower_c = [slot(recv_count) for _ in range(n_rhs)]
    lower_xc = [slot(recv_count) for _ in range(n_rhs)]

    def lower_links(side):
        part = head.at[2, rows_of(side, lane)]
        sends = lower_send[side]
        return (
            link(part, part, r + LANES, c, send=sends[0], recv=lower_recv[side]),
            link(part, part, x_side, c, send=sends[1], recv=lower_x[side]),
            link(part, part, c_side, c, send=sends[2], recv=lower_c[side]),
        )

    def lower_step(turn):
        @pl.when(turn)
        def _():
            for side in range(n_rhs):
                part = head.at[2, rows_of(side, lane)]
                here = is_second & (c == side)

                @pl.when(jnp.logical_not(here))
                def _():
                    arrived(part, lower_recv[side])

                @pl.when(here)
                def _():
                    copy_lower.wait()

                on, across, beside = lower_links(side)

                @pl.when(has_next)
                def _():
                    on.start()

                across.start()
                beside.start()

    @pl.when(passes_points)
    def _():
        for block in range(2):
            @pl.when(lane == block)
            def _():
                points_here(block)
    lower_step(depth == 0)

    @pl.when(updates)
    def _():
        cover(obs_ref, put_base, 0, groups // 2)

    inv_from = [
        (k, lax.rem(c + n_rhs - d, n_rhs)) for k in range(2) for d in range(1, n_rhs)
    ]
    inv_x = [slot(recv_count) for _ in inv_from]
    inv_c = [slot(recv_count) for _ in inv_from]
    inv_xc = [slot(recv_count) for _ in inv_from]
    for n, (k, side) in enumerate(inv_from):
        part = head.at[k, rows_of(side, lane)]
        arrived(part, inv_recv[n])
        forward(part, x_side, inv_x[n]).start()
        forward(part, c_side, inv_c[n]).start()
    lower_step(depth == 1)

    for block in range(2):
        @pl.when(lane != block)
        def _():
            arrived(lead_pts.at[block], point_recv[block])

    cover(lead_pts.at[0], put_first, 0, groups)

    for n, (k, side) in enumerate(inv_from):
        part = head.at[k, rows_of(side, x_lane)]
        arrived(part, inv_x[n])
        forward(part, c_side, inv_xc[n]).start()
    lower_step(depth == 2)

    cover(lead_pts.at[1], put_second, 0, groups)
    lower_step(depth >= 3)

    copy_inv.wait()

    def inverse_here(block):
        for n, (k, side) in enumerate(inv_from):
            if k == block:
                arrived(head.at[k, rows_of(side, c_lane)], inv_c[n])
                arrived(head.at[k, rows_of(side, d_lane)], inv_xc[n])

    inverse_here(0)
    half = solved.shape[2] // 2
    for n in range(2):
        at = slice(n * half, (n + 1) * half)
        solved[0, :, at] = jnp.dot(
            head[0], first_rhs[:, at], preferred_element_type=jnp.float32
        ).astype(jnp.bfloat16)

    for side in range(n_rhs):
        part = head.at[2, rows_of(side, x_lane)]
        arrived(part, lower_x[side])
        forward(part, c_side, lower_xc[side]).start()

    @pl.when(updates)
    def _():
        cover(obs_ref, put_base, groups // 2, groups)

    for side in range(n_rhs):
        arrived(head.at[2, rows_of(side, c_lane)], lower_c[side])
        arrived(head.at[2, rows_of(side, d_lane)], lower_xc[side])
    inverse_here(1)

    for n in range(2):
        at = slice(n * half, (n + 1) * half)
        second_rhs = (second_base[:, at] - jnp.dot(
            head[2], solved[0, :, at], preferred_element_type=jnp.float32
        )).astype(jnp.bfloat16)
        solved[1, :, at] = jnp.dot(
            head[1], second_rhs, preferred_element_type=jnp.float32
        ).astype(jnp.bfloat16)

    copy_tiles.wait()

    def update(at, sem):
        total = base[at, :] - jnp.dot(tiles[0, at, :], solved[0], preferred_element_type=jnp.float32)
        total = total - jnp.dot(tiles[1, at, :], solved[1], preferred_element_type=jnp.float32)
        result[at, :] = total.astype(jnp.bfloat16)
        copy = pltpu.make_async_copy(result.at[at], out_ref.at[0, at], local_sem.at[sem])
        copy.start()
        return copy

    for block in range(2):
        @pl.when(r == block)
        def _():
            copy = pltpu.make_async_copy(solved.at[block], out_ref.at[0], local_sem.at[4])
            copy.start()
            copy.wait()

    @pl.when(updates)
    def _():
        writes = [update(own, 4)]
        sem = 5
        count = 0
        for piece in range(PIECES):
            for d in range(1, n_rhs):
                side = lax.rem(c + n_rhs - d, n_rhs)
                at = pl.ds(pl.multiple_of(side * q + piece * step, step), step)
                arrived(tiles.at[:, at], tile_recv[count])
                writes.append(update(at, sem))
                count += 1
                sem += 1
        for copy in writes:
            copy.wait()
        for copy in tile_copies:
            copy.wait_send()

    for block in range(2):
        @pl.when(r == block)
        def _():
            for copy in far_copies[block]:
                copy.wait_send()

        @pl.when(lane == block)
        def _():
            for copy in mate_copies[block]:
                copy.wait_send()
    for copy in inv_copies + forwards:
        copy.wait_send()
    for source in range(n_rhs):
        @pl.when(is_second & (c == source))
        def _():
            for copy in lower_copies[source]:
                copy.wait_send()
    for side in range(n_rhs):
        on, across, beside = lower_links(side)

        @pl.when(has_next)
        def _():
            on.wait_send()

        across.wait_send()
        beside.wait_send()


def on_device(n_rows, n_rhs, obs_points, pred_points, factor_panels, diag_inverse):
    panels = jnp.transpose(factor_panels[0], (1, 0, 2))
    bs = obs_points.shape[2]
    cols = pred_points.shape[1]
    bf16, f32 = jnp.bfloat16, jnp.float32
    copies = 32 + 2 * n_rows + 16 * n_rhs + 2 * LANES * n_rhs * n_rhs
    return pl.pallas_call(
        functools.partial(kernel, n_rows, n_rhs),
        out_shape=jax.ShapeDtypeStruct((1, bs, cols), bf16),
        in_specs=[
            pl.BlockSpec(memory_space=pltpu.VMEM),
            pl.BlockSpec(memory_space=pltpu.VMEM),
            pl.BlockSpec(memory_space=pl.ANY),
            pl.BlockSpec(memory_space=pl.ANY),
        ],
        out_specs=pl.BlockSpec(memory_space=pl.ANY),
        scratch_shapes=[
            pltpu.VMEM((3, bs, bs), bf16),
            pltpu.VMEM((2, bs, bs), bf16),
            pltpu.VMEM((2, bs, cols), bf16),
            pltpu.VMEM((bs, cols), f32),
            pltpu.VMEM((bs, cols), bf16),
            pltpu.VMEM((bs, cols), f32),
            pltpu.VMEM((2, 8, 2 * bs // 8), jnp.int32),
            pltpu.VMEM((2 * bs // 8, 8), f32),
            pltpu.VMEM((bs, cols), bf16),
            pltpu.SemaphoreType.DMA((8 + PIECES * n_rhs,)),
            pltpu.SemaphoreType.DMA((copies,)),
            pltpu.SemaphoreType.DMA((copies,)),
        ],
        compiler_params=pltpu.CompilerParams(
            collective_id=0, has_side_effects=True, vmem_limit_bytes=40 * 1024 * 1024
        ),
        cost_estimate=pl.CostEstimate(
            flops=10 * bs * bs * cols, bytes_accessed=4 * bs * cols, transcendentals=6 * bs * cols
        ),
    )(obs_points.reshape(8, 2 * bs // 8), pred_points, panels, diag_inverse)


def solution(mesh):
    in_specs = (
        P(None, None, "rows"),
        P(None, "rhs"),
        P(None, ("rows", "rhs"), None, None),
        P(None, "rhs", None),
    )
    body = functools.partial(on_device, mesh.shape["rows"], mesh.shape["rhs"])
    return jax.shard_map(
        body, mesh=mesh, in_specs=in_specs, out_specs=P(None, "rows", "rhs"), check_vma=False
    )
```

```python
import functools
import math

import jax
import jax.numpy as jnp
from jax import lax
from jax.experimental import pallas as pl
from jax.experimental.pallas import tpu as pltpu
from jax.sharding import PartitionSpec as P

SCALE = 16
SILL = 8.0
LANES = 4
PIECES = 2
RATE = math.sqrt(3.0) / SCALE * math.log2(math.e)
SLOPE = SILL * math.log(2.0)
MESH = pl.DeviceIdType.MESH


def covariance(px, py, ox, oy):
    dx = ox - px
    dy = oy - py
    square = dx * dx + dy * dy
    scaled = (square * RATE) * lax.rsqrt(jnp.maximum(square, 1e-6))
    return (SILL + SLOPE * scaled) * jnp.exp2(-scaled)


def kernel(
    n_rows, n_rhs, obs_ref, pred_ref, panel_ref, inv_ref, out_ref,
    head, tiles, solved, base, first_rhs, second_base, lead_pts, columns, result,
    local_sem, send_sem, recv_sem,
):
    r = lax.axis_index("rows")
    c = lax.axis_index("rhs")
    bs = head.shape[1]
    q = bs // n_rhs
    w = q // LANES
    lane = lax.rem(r, LANES)
    hop = r // LANES
    hops = n_rows // LANES
    middle = (hops + 1) // 2
    depth = hop - middle * (hop >= middle).astype(jnp.int32) + (hop >= middle).astype(jnp.int32)
    has_next = (hop < hops - 1) & (hop + 1 != middle)
    has_prev = (hop > 0) & (hop != middle)
    x_side = r + 2 - 4 * (lane // 2)
    c_side = r + 1 - 2 * lax.rem(lane, 2)
    x_lane = lax.rem(x_side, LANES)
    c_lane = lax.rem(c_side, LANES)
    d_lane = lax.rem(c_lane + 2, LANES)
    is_first = r == 0
    is_second = r == 1
    updates = r >= 2

    send_count = [0]
    recv_count = [0]

    def slot(count):
        count[0] += 1
        return count[0] - 1

    def link(src, dst, row, side, send=None, recv=None):
        return pltpu.make_async_remote_copy(
            src_ref=src, dst_ref=dst,
            send_sem=send_sem.at[slot(send_count) if send is None else send],
            recv_sem=recv_sem.at[slot(recv_count) if recv is None else recv],
            device_id=(row, side), device_id_type=MESH,
        )

    def rows_of(side, which):
        return pl.ds(pl.multiple_of(side * q + which * w, w), w)

    def chunk(side):
        return pl.ds(pl.multiple_of(side * q, q), q)

    own = chunk(c)
    copy_inv = pltpu.make_async_copy(inv_ref, head.at[0:2, own], local_sem.at[0])
    copy_tiles = pltpu.make_async_copy(panel_ref, tiles.at[:, own], local_sem.at[1])
    copy_lower = pltpu.make_async_copy(
        panel_ref.at[0, pl.ds(w, w)], head.at[2, rows_of(c, 1)], local_sem.at[2]
    )
    copy_inv.start()
    copy_tiles.start()

    @pl.when(is_second)
    def _():
        copy_lower.start()

    barrier = pltpu.get_barrier_semaphore()

    def greet(row, side):
        pl.semaphore_signal(barrier, inc=1, device_id=(row, side), device_id_type=MESH)

    for d in range(1, n_rhs):
        greet(r, lax.rem(c + d, n_rhs))
    mates = [hop * LANES + lax.rem(lane + d, LANES) for d in range(1, LANES)]
    for mate in mates:
        greet(mate, c)
    passes_points = lane < 2

    @pl.when(has_prev)
    def _():
        greet(r - LANES, c)

    @pl.when((hop > 0) & passes_points)
    def _():
        greet(lane, c)

    @pl.when(hop == middle)
    def _():
        for side in range(n_rhs):
            greet(1, side)

    @pl.when(hop == 0)
    def _():
        for d in range(1, n_rhs):
            greet(1, lax.rem(c + d, n_rhs))

    pl.semaphore_wait(
        barrier,
        n_rhs + LANES - 2
        + has_next.astype(jnp.int32)
        + (r < 2).astype(jnp.int32) * (hops - 1)
        + is_second.astype(jnp.int32) * (LANES * (n_rhs - 1 + n_rhs)),
    )

    inv_copies = []
    inv_recv = []
    for k in range(2):
        for d in range(1, n_rhs):
            inv_recv.append(slot(recv_count))
            copy = link(
                inv_ref.at[k, pl.ds(pl.multiple_of(lane * w, w), w)], head.at[k, rows_of(c, lane)],
                r, lax.rem(c + d, n_rhs), recv=inv_recv[-1],
            )
            copy.start()
            inv_copies.append(copy)

    point_recv = [slot(recv_count) for _ in range(2)]
    far_copies = []
    for block in range(2):
        sends = [
            link(obs_ref, lead_pts.at[block], block + LANES * h, c, recv=point_recv[block])
            for h in range(1, hops)
        ]
        far_copies.append(sends)

        @pl.when(r == block)
        def _():
            for copy in sends:
                copy.start()
    mate_copies = [
        [link(lead_pts.at[block], lead_pts.at[block], mate, c, recv=point_recv[block]) for mate in mates]
        for block in range(2)
    ]

    lower_recv = [slot(recv_count) for _ in range(n_rhs)]
    lower_copies = []
    for source in range(n_rhs):
        sends = [
            link(
                panel_ref.at[0, pl.ds(other * w, w)],
                head.at[2, pl.ds(source * q + other * w, w)],
                middle * LANES + other, side, recv=lower_recv[source],
            )
            for other in range(LANES) for side in range(n_rhs)
        ]
        for other in range(LANES):
            for side in range(n_rhs):
                if (other, side) != (1, source):
                    sends.append(link(
                        panel_ref.at[0, pl.ds(other * w, w)],
                        head.at[2, pl.ds(source * q + other * w, w)],
                        other, side, recv=lower_recv[source],
                    ))
        lower_copies.append(sends)

        @pl.when(is_second & (c == source))
        def _():
            near = sends[LANES * n_rhs:]
            for n, copy in enumerate(sends[:LANES * n_rhs]):
                if n < len(near):
                    near[n].start()
                copy.start()

    step = q // PIECES
    tile_copies = []
    tile_recv = []
    for piece in range(PIECES):
        for d in range(1, n_rhs):
            tile_recv.append(slot(recv_count))
            tile_copies.append(link(
                panel_ref.at[:, pl.ds(piece * step, step)],
                tiles.at[:, pl.ds(pl.multiple_of(c * q + piece * step, step), step)],
                r, lax.rem(c + d, n_rhs), recv=tile_recv[-1],
            ))

    @pl.when(updates)
    def _():
        for copy in tile_copies:
            copy.start()

    px = pred_ref[0:1, :].astype(jnp.float32)
    py = pred_ref[1:2, :].astype(jnp.float32)
    strip = 32
    width = 2 * bs // 8
    groups = bs // width

    def cover(points, store, low, high):
        columns[...] = points[...].astype(jnp.float32).T
        for g in range(low, high):
            @pl.loop(0, width // strip)
            def _(i):
                part = pl.ds(pl.multiple_of(i * strip, strip), strip)
                at = pl.ds(pl.multiple_of(g * width + i * strip, strip), strip)
                ox = columns[part, g:g + 1]
                oy = columns[part, groups + g:groups + g + 1]
                store(at, covariance(px, py, ox, oy))

    def put_base(at, value):
        base[at, :] = value

    def put_first(at, value):
        first_rhs[at, :] = value.astype(jnp.bfloat16)

    def put_second(at, value):
        second_base[at, :] = value

    forwards = []

    def forward(src, row, recv):
        copy = link(src, src, row, c, recv=recv)
        forwards.append(copy)
        return copy

    def arrived(dst, recv):
        link(dst, dst, r, lax.rem(c + 1, n_rhs), send=0, recv=recv).wait_recv()

    def points_here(block):
        @pl.when(r == block)
        def _():
            copy = pltpu.make_async_copy(obs_ref, lead_pts.at[block], local_sem.at[3])
            copy.start()
            copy.wait()

        @pl.when(r != block)
        def _():
            arrived(lead_pts.at[block], point_recv[block])

        @pl.when(lane == block)
        def _():
            for copy in mate_copies[block]:
                copy.start()

    lower_send = [[slot(send_count) for _ in range(3)] for _ in range(n_rhs)]
    lower_x = [slot(recv_count) for _ in range(n_rhs)]
    lower_c = [slot(recv_count) for _ in range(n_rhs)]
    lower_xc = [slot(recv_count) for _ in range(n_rhs)]

    def lower_links(side):
        part = head.at[2, rows_of(side, lane)]
        sends = lower_send[side]
        return (
            link(part, part, r + LANES, c, send=sends[0], recv=lower_recv[side]),
            link(part, part, x_side, c, send=sends[1], recv=lower_x[side]),
            link(part, part, c_side, c, send=sends[2], recv=lower_c[side]),
        )

    def lower_step(turn):
        @pl.when(turn)
        def _():
            for side in range(n_rhs):
                part = head.at[2, rows_of(side, lane)]
                here = is_second & (c == side)

                @pl.when(jnp.logical_not(here))
                def _():
                    arrived(part, lower_recv[side])

                @pl.when(here)
                def _():
                    copy_lower.wait()

                on, across, beside = lower_links(side)

                @pl.when(has_next)
                def _():
                    on.start()

                across.start()
                beside.start()

    @pl.when(passes_points)
    def _():
        for block in range(2):
            @pl.when(lane == block)
            def _():
                points_here(block)
    lower_step(depth == 0)

    @pl.when(updates)
    def _():
        cover(obs_ref, put_base, 0, groups // 2)

    inv_from = [
        (k, lax.rem(c + n_rhs - d, n_rhs)) for k in range(2) for d in range(1, n_rhs)
    ]
    inv_x = [slot(recv_count) for _ in inv_from]
    inv_c = [slot(recv_count) for _ in inv_from]
    inv_xc = [slot(recv_count) for _ in inv_from]
    for n, (k, side) in enumerate(inv_from):
        part = head.at[k, rows_of(side, lane)]
        arrived(part, inv_recv[n])
        forward(part, x_side, inv_x[n]).start()
        forward(part, c_side, inv_c[n]).start()
    lower_step(depth == 1)

    for block in range(2):
        @pl.when(lane != block)
        def _():
            arrived(lead_pts.at[block], point_recv[block])

    cover(lead_pts.at[0], put_first, 0, groups)

    for n, (k, side) in enumerate(inv_from):
        part = head.at[k, rows_of(side, x_lane)]
        arrived(part, inv_x[n])
        forward(part, c_side, inv_xc[n]).start()
    lower_step(depth == 2)

    cover(lead_pts.at[1], put_second, 0, groups)
    lower_step(depth >= 3)

    copy_inv.wait()

    def inverse_here(block):
        for n, (k, side) in enumerate(inv_from):
            if k == block:
                arrived(head.at[k, rows_of(side, c_lane)], inv_c[n])
                arrived(head.at[k, rows_of(side, d_lane)], inv_xc[n])

    inverse_here(0)
    half = solved.shape[2] // 2
    for n in range(2):
        at = slice(n * half, (n + 1) * half)
        solved[0, :, at] = jnp.dot(
            head[0], first_rhs[:, at], preferred_element_type=jnp.float32
        ).astype(jnp.bfloat16)

    for side in range(n_rhs):
        part = head.at[2, rows_of(side, x_lane)]
        arrived(part, lower_x[side])
        forward(part, c_side, lower_xc[side]).start()

    @pl.when(updates)
    def _():
        cover(obs_ref, put_base, groups // 2, groups)

    for side in range(n_rhs):
        arrived(head.at[2, rows_of(side, c_lane)], lower_c[side])
        arrived(head.at[2, rows_of(side, d_lane)], lower_xc[side])
    inverse_here(1)

    for n in range(2):
        at = slice(n * half, (n + 1) * half)
        second_rhs = (second_base[:, at] - jnp.dot(
            head[2], solved[0, :, at], preferred_element_type=jnp.float32
        )).astype(jnp.bfloat16)
        solved[1, :, at] = jnp.dot(
            head[1], second_rhs, preferred_element_type=jnp.float32
        ).astype(jnp.bfloat16)

    copy_tiles.wait()

    def update(at, sem):
        total = base[at, :] - jnp.dot(tiles[0, at, :], solved[0], preferred_element_type=jnp.float32)
        total = total - jnp.dot(tiles[1, at, :], solved[1], preferred_element_type=jnp.float32)
        result[at, :] = total.astype(jnp.bfloat16)
        copy = pltpu.make_async_copy(result.at[at], out_ref.at[0, at], local_sem.at[sem])
        copy.start()
        return copy

    for block in range(2):
        @pl.when(r == block)
        def _():
            copy = pltpu.make_async_copy(solved.at[block], out_ref.at[0], local_sem.at[4])
            copy.start()
            copy.wait()

    @pl.when(updates)
    def _():
        writes = [update(own, 4)]
        sem = 5
        count = 0
        for piece in range(PIECES):
            for d in range(1, n_rhs):
                side = lax.rem(c + n_rhs - d, n_rhs)
                at = pl.ds(pl.multiple_of(side * q + piece * step, step), step)
                arrived(tiles.at[:, at], tile_recv[count])
                writes.append(update(at, sem))
                count += 1
                sem += 1
        for copy in writes:
            copy.wait()
        for copy in tile_copies:
            copy.wait_send()

    for block in range(2):
        @pl.when(r == block)
        def _():
            for copy in far_copies[block]:
                copy.wait_send()

        @pl.when(lane == block)
        def _():
            for copy in mate_copies[block]:
                copy.wait_send()
    for copy in inv_copies + forwards:
        copy.wait_send()
    for source in range(n_rhs):
        @pl.when(is_second & (c == source))
        def _():
            for copy in lower_copies[source]:
                copy.wait_send()
    for side in range(n_rhs):
        on, across, beside = lower_links(side)

        @pl.when(has_next)
        def _():
            on.wait_send()

        across.wait_send()
        beside.wait_send()


def on_device(n_rows, n_rhs, obs_points, pred_points, factor_panels, diag_inverse):
    panels = jnp.transpose(factor_panels[0], (1, 0, 2))
    bs = obs_points.shape[2]
    cols = pred_points.shape[1]
    bf16, f32 = jnp.bfloat16, jnp.float32
    copies = 32 + 2 * n_rows + 16 * n_rhs + 2 * LANES * n_rhs * n_rhs
    return pl.pallas_call(
        functools.partial(kernel, n_rows, n_rhs),
        out_shape=jax.ShapeDtypeStruct((1, bs, cols), bf16),
        in_specs=[
            pl.BlockSpec(memory_space=pltpu.VMEM),
            pl.BlockSpec(memory_space=pltpu.VMEM),
            pl.BlockSpec(memory_space=pl.ANY),
            pl.BlockSpec(memory_space=pl.ANY),
        ],
        out_specs=pl.BlockSpec(memory_space=pl.ANY),
        scratch_shapes=[
            pltpu.VMEM((3, bs, bs), bf16),
            pltpu.VMEM((2, bs, bs), bf16),
            pltpu.VMEM((2, bs, cols), bf16),
            pltpu.VMEM((bs, cols), f32),
            pltpu.VMEM((bs, cols), bf16),
            pltpu.VMEM((bs, cols), f32),
            pltpu.VMEM((2, 8, 2 * bs // 8), jnp.int32),
            pltpu.VMEM((2 * bs // 8, 8), f32),
            pltpu.VMEM((bs, cols), bf16),
            pltpu.SemaphoreType.DMA((8 + PIECES * n_rhs,)),
            pltpu.SemaphoreType.DMA((copies,)),
            pltpu.SemaphoreType.DMA((copies,)),
        ],
        compiler_params=pltpu.CompilerParams(
            collective_id=0, has_side_effects=True, vmem_limit_bytes=40 * 1024 * 1024
        ),
        cost_estimate=pl.CostEstimate(
            flops=10 * bs * bs * cols, bytes_accessed=4 * bs * cols, transcendentals=6 * bs * cols
        ),
    )(obs_points.reshape(8, 2 * bs // 8), pred_points, panels, diag_inverse)


def solution(mesh):
    in_specs = (
        P(None, None, "rows"),
        P(None, "rhs"),
        P(None, ("rows", "rhs"), None, None),
        P(None, "rhs", None),
    )
    body = functools.partial(on_device, mesh.shape["rows"], mesh.shape["rhs"])
    return jax.shard_map(
        body, mesh=mesh, in_specs=in_specs, out_specs=P(None, "rows", "rhs"), check_vma=False
    )
```
